32 devices in a mesh: grp: 2 (over x), wide: 16 (over z, y, core).
Axes of the slice: x: 2, y: 2, z: 4, core: 2. Of those that a mesh axis runs over, the one named last changes fastest.
Arguments:
- raw: bfloat16 [4096, 16, 2048], P(('grp', 'wide')), parts along dimension 0, may hold values from -6 to 6
- cell_feed: int32 [1024], replicated, may hold values from 0 to 1023, each once
- dm_delay: int32 [1024, 1024], replicated, may hold values from 0 to 15
Outputs:
- dedispersed: float32 [2048, 16, 1024], P(('grp', 'wide')), parts along dimension 0
The draws below stay inside these ranges and needn't reach their ends.
There are 2 independent parts, one for each index of `grp`. The reference program is written for one: setup_inputs(seed, part) draws one part's arguments, and reference() takes and returns one part's arrays. A program takes and returns all parts, laid end to end along the dimension named above; an argument that names none is the same for every part. Nothing has to cross between parts.
Inputs may be any that keep to these rules, and one draw needn't show every extreme that they name: `cell_feed`: every antenna stands at exactly one cell.
All inputs are finite; a program needn't handle non-finite values.
Results may differ from the reference program's by a relative error of at most 0.0084.
Values may be sent and summed in bfloat16 or wider, within the bound.
A program may use at most 128 MiB of HBM per device.

```python
import math
import jax
import jax.numpy as jnp
import numpy as np
from jax import lax

NFEED = 2048
NFREQ = 1024
SAMP = 2048
BEAMS = 1024
DMS = 1024
FRAMES = 16


def with_ends(entries, key, least, high):
    extent = entries.shape
    place = [jax.random.randint(jax.random.fold_in(key, axis), (), 0, extent[axis]) for axis in range(len(extent))]
    entries = entries.at[tuple(place)].set(least)
    longest = extent.index(max(extent))
    place[longest] = (place[longest] + 1) % extent[longest]
    return entries.at[tuple(place)].set(high)


def level_of(stream_key, shape, shards, low, largest):
    loudness = 1.0
    for dim, parts in shards:
        draws = jax.random.uniform(jax.random.fold_in(jax.random.fold_in(stream_key, 6), dim), (parts,), jnp.float32, low / len(shards), largest / len(shards))
        loudness = loudness * jnp.repeat(jnp.exp(draws), shape[dim] // parts).reshape((-1,) + (1,) * (len(shape) - 1 - dim))
    return loudness


def scatter_about(key, shape, spread, reach, split=(), kind=jnp.bfloat16):
    values = spread * jax.random.normal(key, shape, jnp.float32)
    if split:
        values = values * level_of(key, shape, split, -0.22, 0.18)
    return jnp.clip(values, -reach, reach).astype(kind)


def setup_inputs(seed: int = 0, part: int = 0) -> dict:
    key_of = jax.random.split(jax.random.key(seed), 4)
    part_splits = jax.random.split(jax.random.fold_in(key_of[3], part), 4)
    raw = scatter_about(part_splits[0], (NFEED, FRAMES, SAMP), 1.0, 6.0, ((0, 16),))
    cell_feed = jax.random.permutation(key_of[1], BEAMS).astype(jnp.int32)
    dm_delay = with_ends(jax.random.randint(key_of[2], (DMS, NFREQ), 0, FRAMES), jax.random.fold_in(key_of[2], 1), 0, FRAMES - 1).astype(jnp.int32)
    return {"raw": raw, "cell_feed": cell_feed, "dm_delay": dm_delay}


EAST_COSINE = np.array([[1, 1, 1, 1], [1, 0, -1, 0], [1, -1, 1, -1], [1, 0, -1, 0]], np.float32)
EAST_SINE = np.array([[0, 0, 0, 0], [0, 1, 0, -1], [0, 0, 0, 0], [0, -1, 0, 1]], np.float32)

def phase_pair(count, length):
    angle = (count % length).astype(jnp.float32) * (2.0 * math.pi / length)
    return (jnp.cos(angle), jnp.sin(angle))

def channel_table(samples, first, width):
    sample_ids = lax.broadcasted_iota(jnp.int32, (samples, width), 0)
    freq_ids = lax.broadcasted_iota(jnp.int32, (samples, width), 1) + first
    cosine, sine = phase_pair(sample_ids * freq_ids, samples)
    factor = 1.0 / math.sqrt(samples)
    return jnp.concatenate([cosine * factor, -sine * factor], axis=1).astype(jnp.bfloat16)

def sky_table(cells):
    rows = lax.broadcasted_iota(jnp.int32, (cells, cells), 0)
    cols = lax.broadcasted_iota(jnp.int32, (cells, cells), 1)
    cosine, sine = phase_pair(rows * cols, cells)
    real_row = jnp.stack([cosine, sine], axis=-1)
    imag_row = jnp.stack([-sine, cosine], axis=-1)
    factor = 1.0 / math.sqrt(cells)
    return (jnp.stack([real_row, imag_row], axis=1) * factor).astype(jnp.bfloat16)

def transform_table(frames):
    terms = frames // 2 + 1
    harmonic = lax.broadcasted_iota(jnp.int32, (terms, frames), 0)
    moment = lax.broadcasted_iota(jnp.int32, (terms, frames), 1)
    cosine, sine = phase_pair(harmonic * moment, frames)
    return jnp.stack([cosine, -sine]).astype(jnp.bfloat16)

def beam_power(spec, feed_index, table):
    grid = jnp.take(spec, feed_index.reshape(-1), axis=0)
    grid = grid.reshape(feed_index.shape + spec.shape[1:])
    beams = jnp.einsum('joni,penrif->poerfj', table.astype(jnp.float32), grid.astype(jnp.float32), precision=lax.Precision.HIGHEST)
    real_part = beams[:, 0]
    imag_part = beams[:, 1]
    cosines = jnp.asarray(EAST_COSINE)
    sines = jnp.asarray(EAST_SINE)
    high = lax.Precision.HIGHEST
    east_real = 0.5 * (jnp.einsum('qe,perfj->prfqj', cosines, real_part, precision=high) + jnp.einsum('qe,perfj->prfqj', sines, imag_part, precision=high))
    east_imag = 0.5 * (jnp.einsum('qe,perfj->prfqj', cosines, imag_part, precision=high) - jnp.einsum('qe,perfj->prfqj', sines, real_part, precision=high))
    power = 0.5 * lax.optimization_barrier(jnp.sum(east_real * east_real + east_imag * east_imag, axis=0))
    return power.reshape(power.shape[0], power.shape[1], -1)

def reference(raw, cell_feed, dm_delay):
    nfeed, frames, samples = raw.shape
    nfreq = samples // 2
    fblock = math.gcd(nfreq, 64)
    cells = cell_feed.shape[0] // 4
    polar = lax.broadcasted_iota(jnp.int32, (2, 4, cells), 0)
    feed_index = 2 * cell_feed.reshape(1, 4, cells).astype(jnp.int32) + polar
    table_sky = sky_table(cells)
    flat = raw.reshape(nfeed * frames, samples).astype(jnp.float32)

    def one_block(index):
        table = channel_table(samples, index * fblock, fblock).astype(jnp.float32)
        spectra = jnp.dot(flat, table, precision=lax.Precision.HIGHEST).astype(jnp.bfloat16)
        return beam_power(spectra.reshape(nfeed, frames, 2, fblock), feed_index, table_sky)
    power = lax.map(one_block, jnp.arange(nfreq // fblock, dtype=jnp.int32))
    power = jnp.moveaxis(power, 0, 1).reshape(frames, nfreq, -1)
    intensity = (power - lax.optimization_barrier(jnp.mean(power, axis=0, keepdims=True))).astype(jnp.bfloat16)
    spectrum = jnp.einsum('okr,rfb->kofb', transform_table(frames).astype(jnp.float32), intensity.astype(jnp.float32), precision=lax.Precision.HIGHEST).astype(jnp.bfloat16)

    def one_term(term):
        harmonic, block = term
        cosine, sine = phase_pair(harmonic * dm_delay, frames)
        factors = jnp.stack([cosine, sine]).astype(jnp.bfloat16).astype(jnp.float32)
        products = jnp.einsum('ofb,udf->boud', block.astype(jnp.float32), factors, precision=lax.Precision.HIGHEST)
        real_part = products[:, 0, 0] - products[:, 1, 1]
        imag_part = products[:, 0, 1] + products[:, 1, 0]
        return jnp.stack([real_part, imag_part], axis=1)
    terms = frames // 2 + 1
    trials = lax.map(one_term, (jnp.arange(terms, dtype=jnp.int32), spectrum))
    moment = lax.broadcasted_iota(jnp.int32, (frames, terms), 0)
    harmonic = lax.broadcasted_iota(jnp.int32, (frames, terms), 1)
    cosine, sine = phase_pair(moment * harmonic, frames)
    weight = jnp.where((harmonic == 0) | (harmonic * 2 == frames), 1.0, 2.0).astype(jnp.float32)
    weight = weight / (frames * math.sqrt(nfreq))
    table = jnp.stack([cosine * weight, -sine * weight], axis=1)
    return jnp.einsum('tuk,kbud->btd', table, trials, precision=lax.Precision.HIGHEST)
```

```python
import functools
import math

import jax
import jax.numpy as jnp
import ml_dtypes
import numpy as np
from jax import lax
from jax.experimental import pallas as pl
from jax.experimental.pallas import tpu as pltpu
from jax.sharding import PartitionSpec as P

BF16 = jnp.bfloat16
F32 = jnp.float32
PARAMS = pltpu.CompilerParams(vmem_limit_bytes=56 * 2**20)


def channel_rows(samples, chunks):
    nfreq = samples // 2
    turns = (np.arange(nfreq)[:, None] * np.arange(samples)[None, :]) % samples
    angle = turns * (2.0 * math.pi / samples)
    table = np.stack([np.cos(angle), -np.sin(angle)]) / math.sqrt(samples)
    table = table.reshape(2, chunks, nfreq // chunks, samples).transpose(1, 0, 2, 3)
    return table.reshape(chunks, -1, samples).astype(ml_dtypes.bfloat16)


def frame_factors(frames):
    angle = 2.0 * math.pi * (np.outer(np.arange(frames), np.arange(frames)) % frames) / frames
    rounded = lambda v: np.round(v, 12).astype(ml_dtypes.bfloat16).astype(np.float64)
    return rounded(np.cos(angle)), rounded(-np.sin(angle))


def sky_matrix(cell_feed, devices):
    total = cell_feed.shape[0]
    cells = total // 4
    per = total // devices
    places = lax.broadcasted_iota(jnp.int32, (total, total), 1)
    feeds = lax.broadcasted_iota(jnp.int32, (total, total), 0)
    cell = jnp.sum(jnp.where(cell_feed[None, :] == feeds, places, 0), axis=1)
    row = (cell % cells).reshape(devices, 1, per, 1, 1)
    col = (cell // cells).reshape(devices, 1, per, 1, 1)
    shape = (devices, 2, per, 2, total)
    beam = lax.broadcasted_iota(jnp.int32, (1, 1, 1, 1, total), 4)
    part_in = lax.broadcasted_iota(jnp.int32, (1, 2, 1, 1, 1), 1)
    part_out = lax.broadcasted_iota(jnp.int32, (1, 1, 1, 2, 1), 3)
    quarter = cells // 4
    turns = (beam % cells) * row + quarter * ((beam // cells) * col + part_out - part_in + 4)
    angle = (turns % cells).astype(F32) * (2.0 * math.pi / cells)
    table = (jnp.cos(angle) * (1.0 / math.sqrt(cells))).astype(BF16)
    return jnp.broadcast_to(table, shape).reshape(2 * total, 2 * total)


def split_halves(a, b):
    half = a.shape[-1] // 2
    low = lax.broadcasted_iota(jnp.int32, a.shape, a.ndim - 1) < half
    return (
        jnp.where(low, a, pltpu.roll(b, half, a.ndim - 1)),
        jnp.where(low, pltpu.roll(a, half, a.ndim - 1), b),
    )


def reorder_kernel(perm_ref, raw_ref, out_ref):
    block, frames, samples = raw_ref.shape
    rows = raw_ref[...].reshape(block * frames, samples)
    moved = jnp.dot(perm_ref[...], rows, preferred_element_type=F32).astype(BF16)
    out_ref[...] = moved.reshape(out_ref.shape)


def reorder(raw, fast):
    feeds, frames, samples = raw.shape
    ants = feeds // 2
    if not fast:
        out = raw.reshape(ants, 2, frames, samples).transpose(2, 1, 0, 3)
        return out.reshape(feeds * frames, samples)
    block = 16
    size = 2 * block * frames
    target = np.arange(size).reshape(block, 2, frames).transpose(2, 1, 0).reshape(-1)
    perm = np.zeros((size, size), ml_dtypes.bfloat16)
    perm[np.arange(size), target] = 1
    width = samples // 2
    out = pl.pallas_call(
        reorder_kernel,
        grid=(ants // block, 2),
        in_specs=[
            pl.BlockSpec((size, size), lambda i, j: (0, 0)),
            pl.BlockSpec((2 * block, frames, width), lambda i, j: (i, 0, j)),
        ],
        out_specs=pl.BlockSpec((frames, 2, block, width), lambda i, j: (0, 0, i, j)),
        out_shape=jax.ShapeDtypeStruct((frames, 2, ants, samples), BF16),
        compiler_params=PARAMS,
        name="reorder",
    )(jnp.asarray(perm), raw)
    return out.reshape(feeds * frames, samples)


def channel_kernel(table_ref, rows_ref, out_ref):
    devices, _, frames, freqs, lanes = out_ref.shape
    half = table_ref.shape[0] // 2
    for r in range(frames):
        spec = lax.dot_general(
            table_ref[...],
            rows_ref[r * lanes : (r + 1) * lanes, :],
            (((1,), (1,)), ((), ())),
            preferred_element_type=F32,
        )
        pair = split_halves(spec[:half], spec[half:])
        for p in range(2):
            out_ref[:, p, r] = pair[p].astype(BF16).reshape(devices, freqs, lanes)


def channelise(rows, table, devices, frames, fast):
    total, samples = rows.shape
    ants = total // (2 * frames)
    freqs = table.shape[0] // (2 * devices)
    if not fast:
        spec = lax.dot_general(
            table, rows, (((1,), (1,)), ((), ())), preferred_element_type=F32
        ).astype(BF16)
        spec = spec.reshape(2, devices, freqs, frames, 2, ants).transpose(1, 4, 3, 2, 0, 5)
        return spec.reshape(devices, 2, frames, freqs, 2 * ants)
    block = 4
    return pl.pallas_call(
        channel_kernel,
        grid=(frames // block,),
        in_specs=[
            pl.BlockSpec(table.shape, lambda i: (0, 0)),
            pl.BlockSpec((block * 2 * ants, samples), lambda i: (i, 0)),
        ],
        out_specs=pl.BlockSpec(
            (devices, 2, block, freqs, 2 * ants), lambda i: (0, 0, i, 0, 0)
        ),
        out_shape=jax.ShapeDtypeStruct((devices, 2, frames, freqs, 2 * ants), BF16),
        compiler_params=PARAMS,
        name="channelise",
    )(table, rows)


def harmonics_of(power, frames):
    mean = functools.reduce(lambda x, y: x + y, power) * (1.0 / frames)
    rows = [(v - mean).astype(BF16).astype(F32) for v in power]
    cosine, sine = frame_factors(frames)

    def total(weights):
        terms = [float(w) * v for w, v in zip(weights, rows) if w != 0]
        return functools.reduce(lambda x, y: x + y, terms)

    planes = [(total(cosine[0]), total(cosine[frames // 2]))]
    for h in range(1, frames // 2):
        planes.append((total(cosine[h]), total(sine[h])))
    return planes


def beam_kernel(spec_ref, real_ref, imag_ref, out_ref, left):
    devices, _, frames, freqs, lanes = spec_ref.shape
    rows = 2 * frames * freqs

    @pl.when(pl.program_id(0) == 0)
    def _():
        for w in range(devices):
            left[:, w * lanes : (w + 1) * lanes] = spec_ref[w].reshape(rows, lanes)

    real = jnp.dot(left[...], real_ref[...], preferred_element_type=F32)
    imag = jnp.dot(left[...], imag_ref[...], preferred_element_type=F32)
    square = (real * real + imag * imag).reshape(2, frames, freqs, -1)
    power = (square[0] + square[1]) * 0.125
    planes = harmonics_of([power[r] for r in range(frames)], frames)
    for h, (a, b) in enumerate(planes):
        for g in range(out_ref.shape[0] // 2):
            cut = slice(g * lanes, (g + 1) * lanes)
            first, second = split_halves(a[:, cut], b[:, cut])
            out_ref[2 * g, h] = first.astype(BF16)
            out_ref[2 * g + 1, h] = second.astype(BF16)


def beamform(spec, matrix, fast):
    devices, _, frames, freqs, lanes = spec.shape
    total = matrix.shape[1] // 2
    per = total // devices
    planes = frames // 2
    if not fast:
        beams = jnp.einsum(
            "wprfx,wxub->prfub",
            spec,
            matrix.reshape(devices, lanes, 2, total),
            preferred_element_type=F32,
        )
        power = 0.125 * jnp.sum(beams * beams, axis=(0, 3))
        found = harmonics_of([power[r] for r in range(frames)], frames)
        out = jnp.stack([jnp.stack(pair) for pair in found]).astype(BF16)
        out = out.reshape(planes, 2, freqs, devices, per).transpose(3, 0, 2, 1, 4)
        return out.reshape(devices, planes, freqs, 2 * per)
    steps = 4
    width = total // steps
    return pl.pallas_call(
        beam_kernel,
        grid=(steps,),
        in_specs=[
            pl.BlockSpec(spec.shape, lambda i: (0, 0, 0, 0, 0)),
            pl.BlockSpec((matrix.shape[0], width), lambda i: (0, i)),
            pl.BlockSpec((matrix.shape[0], width), lambda i: (0, i + steps)),
        ],
        out_specs=pl.BlockSpec(
            (devices // steps, planes, freqs, 2 * per), lambda i: (i, 0, 0, 0)
        ),
        out_shape=jax.ShapeDtypeStruct((devices, planes, freqs, 2 * per), BF16),
        scratch_shapes=[pltpu.VMEM((2 * frames * freqs, devices * lanes), BF16)],
        compiler_params=PARAMS,
        name="beamform",
    )(spec, matrix, matrix)


def trial_planes(block, cosine, sine, before):
    devices, planes, freqs, lanes = block.shape
    half = lanes // 2
    low = lax.broadcasted_iota(jnp.int32, (devices * freqs, lanes), 1) < half
    turn = lambda c, s: (c * cosine - s * sine, s * cosine + c * sine)
    result = []
    now = (cosine, sine)
    for h in [*range(1, planes), 0]:
        left = block[:, h].reshape(devices * freqs, lanes).astype(F32)
        if h:
            other = jnp.concatenate([-left[:, half:], left[:, :half]], axis=1)
            right = (now[0].astype(BF16), now[1].astype(BF16))
            now = turn(*now)
        else:
            other = jnp.where(low, 0.0, left)
            left = jnp.where(low, left, 0.0)
            right = (jnp.ones(cosine.shape, BF16), now[0].astype(BF16))
        sums = lax.dot_general(
            jnp.concatenate([left, other], axis=0).astype(BF16),
            jnp.concatenate(right, axis=0),
            (((0,), (0,)), ((), ())),
            preferred_element_type=F32,
        )
        result.append((h, sums if before is None else sums + before[h]))
    return [plane for _, plane in sorted(result, key=lambda item: item[0])]


def synthesis(planes, frames, nfreq):
    half = planes[0].shape[0] // 2
    scale = 1.0 / (frames * math.sqrt(nfreq))
    middle = frames // 2
    real = {0: planes[0][:half] * scale, middle: planes[0][half:] * scale}
    imag = {}
    for h in range(1, middle):
        real[h] = planes[h][:half] * (2.0 * scale)
        imag[h] = planes[h][half:] * (2.0 * scale)
    add = lambda terms: functools.reduce(lambda x, y: x + y, terms)

    def weighted(values, t, parity, wave):
        found = []
        for h, v in values.items():
            factor = round(wave(2.0 * math.pi * ((h * t) % frames) / frames), 15)
            if h % 2 == parity and factor != 0:
                found.append(v if factor == 1 else -v if factor == -1 else v * factor)
        return add(found) if found else jnp.zeros_like(real[0])

    out = [None] * frames
    for t in range(middle // 2 + 1):
        even, odd = (weighted(real, t, p, math.cos) for p in range(2))
        even_s, odd_s = (weighted(imag, t, p, math.sin) for p in range(2))
        for at, a, b in ((t, even + odd, even_s + odd_s), (middle - t, even - odd, odd_s - even_s)):
            out[at] = a - b
            out[(frames - at) % frames] = a + b if at % middle else a - b
    return out


def trial_kernel(last, nfreq, frames, *refs):
    block_ref, cos_ref, sin_ref, *rest = refs
    before = rest[0] if len(rest) == 2 else None
    out_ref = rest[-1]
    found = trial_planes(block_ref[...], cos_ref[...], sin_ref[...], before)
    if not last:
        for h, plane in enumerate(found):
            out_ref[h] = plane
        return
    beams = out_ref.shape[0] // frames
    for t, series in enumerate(synthesis(found, frames, nfreq)):
        out_ref[pl.ds(t, beams, stride=frames), :] = series


def dedisperse(block, cosine, sine, chunk, before, last, nfreq, frames, fast):
    devices, planes, freqs, lanes = block.shape
    depth = devices * freqs
    trials = cosine.shape[1]
    beams = lanes // 2
    if not fast:
        cut = slice(chunk * depth, (chunk + 1) * depth)
        found = trial_planes(block, cosine[cut], sine[cut], before)
        if not last:
            return jnp.stack(found)
        return jnp.stack(synthesis(found, frames, nfreq), axis=1)
    width = min(128, trials)
    in_specs = [
        pl.BlockSpec(block.shape, lambda i: (0, 0, 0, 0)),
        pl.BlockSpec((depth, width), lambda i: (chunk, i)),
        pl.BlockSpec((depth, width), lambda i: (chunk, i)),
    ]
    args = [block, cosine, sine]
    if before is not None:
        in_specs.append(pl.BlockSpec((planes, lanes, width), lambda i: (0, 0, i)))
        args.append(before)
    if last:
        out_spec = pl.BlockSpec((beams * frames, width), lambda i: (0, i))
        out_shape = jax.ShapeDtypeStruct((beams * frames, trials), F32)
    else:
        out_spec = pl.BlockSpec((planes, lanes, width), lambda i: (0, 0, i))
        out_shape = jax.ShapeDtypeStruct((planes, lanes, trials), F32)
    out = pl.pallas_call(
        functools.partial(trial_kernel, last, nfreq, frames),
        grid=(trials // width,),
        in_specs=in_specs,
        out_specs=out_spec,
        out_shape=out_shape,
        compiler_params=PARAMS,
        name="dedisperse_last" if last else "dedisperse",
    )(*args)
    return out.reshape(beams, frames, trials) if last else out


def body(devices, raw, cell_feed, dm_delay):
    feeds, frames, samples = raw.shape
    nfreq = samples // 2
    chunks = math.gcd(4, nfreq // devices)
    freqs = nfreq // (devices * chunks)
    per = cell_feed.shape[0] // devices
    fast = (
        feeds == 128 and per == 64 and freqs % 16 == 0 and frames == 16 and devices % 8 == 0
    )
    table = channel_rows(samples, chunks)
    exchange = lambda v: lax.all_to_all(v, "wide", split_axis=0, concat_axis=0, tiled=True)
    rows = reorder(raw, fast)
    sent = [channelise(rows, jnp.asarray(table[c]), devices, frames, fast) for c in range(chunks)]
    arrived = [exchange(v) for v in sent]
    matrix = sky_matrix(cell_feed, devices)
    angle = (jnp.transpose(dm_delay) % frames).astype(F32) * (2.0 * math.pi / frames)
    cosine, sine = jnp.cos(angle), jnp.sin(angle)
    spectrum = [exchange(beamform(v, matrix, fast)) for v in arrived]
    total = None
    for c in range(chunks):
        total = dedisperse(
            spectrum[c], cosine, sine, c, total, c == chunks - 1, nfreq, frames, fast
        )
    return total


def solution(mesh):
    placed = (P(("grp", "wide"), None, None), P(), P())
    return jax.shard_map(
        functools.partial(body, mesh.shape["wide"]),
        mesh=mesh,
        in_specs=placed,
        out_specs=P(("grp", "wide"), None, None),
        check_vma=False,
    )
```

```python
import functools
import math

import jax
import jax.numpy as jnp
import ml_dtypes
import numpy as np
from jax import lax
from jax.experimental import pallas as pl
from jax.experimental.pallas import tpu as pltpu
from jax.sharding import PartitionSpec as P

BF16 = jnp.bfloat16
F32 = jnp.float32
PARAMS = pltpu.CompilerParams(vmem_limit_bytes=56 * 2**20)


def channel_rows(samples, chunks):
    nfreq = samples // 2
    turns = (np.arange(nfreq)[:, None] * np.arange(samples)[None, :]) % samples
    angle = turns * (2.0 * math.pi / samples)
    table = np.stack([np.cos(angle), -np.sin(angle)]) / math.sqrt(samples)
    table = table.reshape(2, chunks, nfreq // chunks, samples).transpose(1, 0, 2, 3)
    return table.reshape(chunks, -1, samples).astype(ml_dtypes.bfloat16)


def frame_factors(frames):
    angle = 2.0 * math.pi * (np.outer(np.arange(frames), np.arange(frames)) % frames) / frames
    rounded = lambda v: np.round(v, 12).astype(ml_dtypes.bfloat16).astype(np.float64)
    return rounded(np.cos(angle)), rounded(-np.sin(angle))


def sky_kernel(cosine_ref, sine_ref, row_ref, col_ref, out_ref):
    per = row_ref.shape[0]
    cells = cosine_ref.shape[0]
    here = lax.broadcasted_iota(jnp.int32, (per, cells), 1) == row_ref[...]
    pick = jnp.where(here, 1.0, 0.0).astype(BF16)
    cosine = jnp.dot(pick, cosine_ref[...], preferred_element_type=F32)
    minus = -jnp.dot(pick, sine_ref[...], preferred_element_type=F32)
    for part in range(2):
        for out in range(2):
            for q in range(4):
                turn = (col_ref[...] * q + (out - part + 4)) & 3
                turn = jnp.broadcast_to(turn, cosine.shape)
                value = jnp.where((turn & 1) == 1, minus, cosine)
                value = jnp.where(turn >= 2, -value, value).astype(BF16)
                at = (out * 4 + q) * cells
                out_ref[part * per : (part + 1) * per, at : at + cells] = value


def sky_matrix(cell_feed, devices, fast):
    total = cell_feed.shape[0]
    cells = total // 4
    per = total // devices
    places = lax.broadcasted_iota(jnp.int32, (total, total), 1)
    feeds = lax.broadcasted_iota(jnp.int32, (total, total), 0)
    cell = jnp.sum(jnp.where(cell_feed[None, :] == feeds, places, 0), axis=1, keepdims=True)
    row = cell % cells
    col = cell // cells
    if fast:
        turns = np.outer(np.arange(cells), np.arange(cells)) % cells
        angle = turns * (2.0 * math.pi / cells)
        tables = [
            jnp.asarray((wave(angle) / math.sqrt(cells)).astype(ml_dtypes.bfloat16))
            for wave in (np.cos, np.sin)
        ]
        return pl.pallas_call(
            sky_kernel,
            grid=(devices,),
            in_specs=[
                pl.BlockSpec((cells, cells), lambda i: (0, 0)),
                pl.BlockSpec((cells, cells), lambda i: (0, 0)),
                pl.BlockSpec((per, 1), lambda i: (i, 0)),
                pl.BlockSpec((per, 1), lambda i: (i, 0)),
            ],
            out_specs=pl.BlockSpec((2 * per, 2 * total), lambda i: (i, 0)),
            out_shape=jax.ShapeDtypeStruct((2 * total, 2 * total), BF16),
            compiler_params=PARAMS,
            name="sky",
        )(*tables, row, col)
    row = row.reshape(devices, 1, per, 1, 1)
    col = col.reshape(devices, 1, per, 1, 1)
    shape = (devices, 2, per, 2, total)
    beam = lax.broadcasted_iota(jnp.int32, (1, 1, 1, 1, total), 4)
    part_in = lax.broadcasted_iota(jnp.int32, (1, 2, 1, 1, 1), 1)
    part_out = lax.broadcasted_iota(jnp.int32, (1, 1, 1, 2, 1), 3)
    quarter = cells // 4
    turns = (beam % cells) * row + quarter * ((beam // cells) * col + part_out - part_in + 4)
    angle = (turns % cells).astype(F32) * (2.0 * math.pi / cells)
    table = (jnp.cos(angle) * (1.0 / math.sqrt(cells))).astype(BF16)
    return jnp.broadcast_to(table, shape).reshape(2 * total, 2 * total)


def split_halves(a, b):
    half = a.shape[-1] // 2
    low = lax.broadcasted_iota(jnp.int32, a.shape, a.ndim - 1) < half
    return (
        jnp.where(low, a, pltpu.roll(b, half, a.ndim - 1)),
        jnp.where(low, pltpu.roll(a, half, a.ndim - 1), b),
    )


def reorder_kernel(perm_ref, raw_ref, out_ref):
    block, frames, samples = raw_ref.shape
    size = perm_ref.shape[0]
    rows = raw_ref[...].reshape(block * frames, samples)
    parts = [
        jnp.dot(perm_ref[...], rows[at : at + size], preferred_element_type=F32)
        for at in range(0, block * frames, size)
    ]
    parts = [v.reshape(2 * frames, size // (2 * frames), samples) for v in parts]
    moved = jnp.concatenate(parts, axis=1).astype(BF16)
    out_ref[...] = moved.reshape(out_ref.shape)


def reorder(raw, fast):
    feeds, frames, samples = raw.shape
    ants = feeds // 2
    if not fast:
        out = raw.reshape(ants, 2, frames, samples).transpose(2, 1, 0, 3)
        return out.reshape(feeds * frames, samples)
    block = 16
    size = block * frames
    target = np.arange(size).reshape(block // 2, 2, frames).transpose(2, 1, 0).reshape(-1)
    perm = np.zeros((size, size), ml_dtypes.bfloat16)
    perm[np.arange(size), target] = 1
    width = samples // 2
    out = pl.pallas_call(
        reorder_kernel,
        grid=(ants // block, 2),
        in_specs=[
            pl.BlockSpec((size, size), lambda i, j: (0, 0)),
            pl.BlockSpec((2 * block, frames, width), lambda i, j: (i, 0, j)),
        ],
        out_specs=pl.BlockSpec((frames, 2, block, width), lambda i, j: (0, 0, i, j)),
        out_shape=jax.ShapeDtypeStruct((frames, 2, ants, samples), BF16),
        compiler_params=PARAMS,
        name="reorder",
    )(jnp.asarray(perm), raw)
    return out.reshape(feeds * frames, samples)


def channel_kernel(table_ref, rows_ref, out_ref):
    devices, _, frames, freqs, lanes = out_ref.shape
    half = table_ref.shape[0] // 2
    whole = lax.dot_general(
        table_ref[...], rows_ref[...], (((1,), (1,)), ((), ())), preferred_element_type=F32
    )
    for r in range(frames):
        spec = whole[:, r * lanes : (r + 1) * lanes]
        pair = split_halves(spec[:half], spec[half:])
        for p in range(2):
            out_ref[:, p, r] = pair[p].astype(BF16).reshape(devices, freqs, lanes)


def channelise(rows, table, devices, frames, fast):
    total, samples = rows.shape
    ants = total // (2 * frames)
    freqs = table.shape[0] // (2 * devices)
    if not fast:
        spec = lax.dot_general(
            table, rows, (((1,), (1,)), ((), ())), preferred_element_type=F32
        ).astype(BF16)
        spec = spec.reshape(2, devices, freqs, frames, 2, ants).transpose(1, 4, 3, 2, 0, 5)
        return spec.reshape(devices, 2, frames, freqs, 2 * ants)
    block = 4
    return pl.pallas_call(
        channel_kernel,
        grid=(frames // block,),
        in_specs=[
            pl.BlockSpec(table.shape, lambda i: (0, 0)),
            pl.BlockSpec((block * 2 * ants, samples), lambda i: (i, 0)),
        ],
        out_specs=pl.BlockSpec(
            (devices, 2, block, freqs, 2 * ants), lambda i: (0, 0, i, 0, 0)
        ),
        out_shape=jax.ShapeDtypeStruct((devices, 2, frames, freqs, 2 * ants), BF16),
        compiler_params=PARAMS,
        name="channelise",
    )(table, rows)


def harmonics_of(power, frames):
    mean = functools.reduce(lambda x, y: x + y, power) * (1.0 / frames)
    rows = [(v - mean).astype(BF16).astype(F32) for v in power]
    cosine, sine = frame_factors(frames)

    def total(weights):
        terms = [float(w) * v for w, v in zip(weights, rows) if w != 0]
        return functools.reduce(lambda x, y: x + y, terms)

    planes = [(total(cosine[0]), total(cosine[frames // 2]))]
    for h in range(1, frames // 2):
        planes.append((total(cosine[h]), total(sine[h])))
    return planes


def beam_kernel(spec_ref, real_ref, imag_ref, out_ref, left):
    devices, _, frames, freqs, lanes = spec_ref.shape
    rows = 2 * frames * freqs

    @pl.when(pl.program_id(0) == 0)
    def _():
        for w in range(devices):
            left[:, w * lanes : (w + 1) * lanes] = spec_ref[w].reshape(rows, lanes)

    real = jnp.dot(left[...], real_ref[...], preferred_element_type=F32)
    imag = jnp.dot(left[...], imag_ref[...], preferred_element_type=F32)
    square = (real * real + imag * imag).reshape(2, frames, freqs, -1)
    power = (square[0] + square[1]) * 0.125
    planes = harmonics_of([power[r] for r in range(frames)], frames)
    for h, (a, b) in enumerate(planes):
        for g in range(out_ref.shape[0] // 2):
            cut = slice(g * lanes, (g + 1) * lanes)
            first, second = split_halves(a[:, cut], b[:, cut])
            out_ref[2 * g, h] = first.astype(BF16)
            out_ref[2 * g + 1, h] = second.astype(BF16)


def beamform(spec, matrix, fast):
    devices, _, frames, freqs, lanes = spec.shape
    total = matrix.shape[1] // 2
    per = total // devices
    planes = frames // 2
    if not fast:
        beams = jnp.einsum(
            "wprfx,wxub->prfub",
            spec,
            matrix.reshape(devices, lanes, 2, total),
            preferred_element_type=F32,
        )
        power = 0.125 * jnp.sum(beams * beams, axis=(0, 3))
        found = harmonics_of([power[r] for r in range(frames)], frames)
        out = jnp.stack([jnp.stack(pair) for pair in found]).astype(BF16)
        out = out.reshape(planes, 2, freqs, devices, per).transpose(3, 0, 2, 1, 4)
        return out.reshape(devices, planes, freqs, 2 * per)
    steps = 4
    width = total // steps
    return pl.pallas_call(
        beam_kernel,
        grid=(steps,),
        in_specs=[
            pl.BlockSpec(spec.shape, lambda i: (0, 0, 0, 0, 0)),
            pl.BlockSpec((matrix.shape[0], width), lambda i: (0, i)),
            pl.BlockSpec((matrix.shape[0], width), lambda i: (0, i + steps)),
        ],
        out_specs=pl.BlockSpec(
            (devices // steps, planes, freqs, 2 * per), lambda i: (i, 0, 0, 0)
        ),
        out_shape=jax.ShapeDtypeStruct((devices, planes, freqs, 2 * per), BF16),
        scratch_shapes=[pltpu.VMEM((2 * frames * freqs, devices * lanes), BF16)],
        compiler_params=PARAMS,
        name="beamform",
    )(spec, matrix, matrix)


def trial_planes(block, cosine, sine, before):
    devices, planes, freqs, lanes = block.shape
    half = lanes // 2
    low = lax.broadcasted_iota(jnp.int32, (devices * freqs, lanes), 1) < half
    turn = lambda c, s: (c * cosine - s * sine, s * cosine + c * sine)
    result = []
    now = (cosine, sine)
    for h in [*range(1, planes), 0]:
        left = block[:, h].reshape(devices * freqs, lanes).astype(F32)
        if h:
            other = jnp.concatenate([-left[:, half:], left[:, :half]], axis=1)
            right = (now[0].astype(BF16), now[1].astype(BF16))
            now = turn(*now)
        else:
            other = jnp.where(low, 0.0, left)
            left = jnp.where(low, left, 0.0)
            right = (jnp.ones(cosine.shape, BF16), now[0].astype(BF16))
        sums = lax.dot_general(
            jnp.concatenate([left, other], axis=0).astype(BF16),
            jnp.concatenate(right, axis=0),
            (((0,), (0,)), ((), ())),
            preferred_element_type=F32,
        )
        result.append((h, sums if before is None else sums + before[h]))
    return [plane for _, plane in sorted(result, key=lambda item: item[0])]


def synthesis(planes, frames, nfreq):
    half = planes[0].shape[0] // 2
    scale = 1.0 / (frames * math.sqrt(nfreq))
    middle = frames // 2
    real = {0: planes[0][:half] * scale, middle: planes[0][half:] * scale}
    imag = {}
    for h in range(1, middle):
        real[h] = planes[h][:half] * (2.0 * scale)
        imag[h] = planes[h][half:] * (2.0 * scale)
    add = lambda terms: functools.reduce(lambda x, y: x + y, terms)

    def weighted(values, t, parity, wave):
        found = []
        for h, v in values.items():
            factor = round(wave(2.0 * math.pi * ((h * t) % frames) / frames), 15)
            if h % 2 == parity and factor != 0:
                found.append(v if factor == 1 else -v if factor == -1 else v * factor)
        return add(found) if found else jnp.zeros_like(real[0])

    out = [None] * frames
    for t in range(middle // 2 + 1):
        even, odd = (weighted(real, t, p, math.cos) for p in range(2))
        even_s, odd_s = (weighted(imag, t, p, math.sin) for p in range(2))
        for at, a, b in ((t, even + odd, even_s + odd_s), (middle - t, even - odd, odd_s - even_s)):
            out[at] = a - b
            out[(frames - at) % frames] = a + b if at % middle else a - b
    return out


def trial_kernel(last, nfreq, frames, *refs):
    block_ref, cos_ref, sin_ref, *rest = refs
    found = rest[0] if len(rest) == 2 else None
    out_ref = rest[-1]
    devices, count, _, freqs, _ = block_ref.shape
    depth = devices * freqs
    for c in range(count):
        cut = slice(c * depth, (c + 1) * depth)
        found = trial_planes(block_ref[:, c], cos_ref[cut, :], sin_ref[cut, :], found)
    if not last:
        for h, plane in enumerate(found):
            out_ref[h] = plane
        return
    beams = out_ref.shape[0] // frames
    for t, series in enumerate(synthesis(found, frames, nfreq)):
        out_ref[pl.ds(t, beams, stride=frames), :] = series


def dedisperse(block, cosine, sine, first, before, last, nfreq, frames, fast):
    devices, count, planes, freqs, lanes = block.shape
    depth = devices * freqs
    trials = cosine.shape[1]
    beams = lanes // 2
    if not fast:
        found = before
        for c in range(count):
            cut = slice((first + c) * depth, (first + c + 1) * depth)
            found = trial_planes(block[:, c], cosine[cut], sine[cut], found)
        if not last:
            return jnp.stack(found)
        return jnp.stack(synthesis(found, frames, nfreq), axis=1)
    width = min(128 if last else 256, trials)
    at = first // count
    in_specs = [
        pl.BlockSpec(block.shape, lambda i: (0, 0, 0, 0, 0)),
        pl.BlockSpec((count * depth, width), lambda i: (at, i)),
        pl.BlockSpec((count * depth, width), lambda i: (at, i)),
    ]
    args = [block, cosine, sine]
    if before is not None:
        in_specs.append(pl.BlockSpec((planes, lanes, width), lambda i: (0, 0, i)))
        args.append(before)
    if last:
        out_spec = pl.BlockSpec((beams * frames, width), lambda i: (0, i))
        out_shape = jax.ShapeDtypeStruct((beams * frames, trials), F32)
    else:
        out_spec = pl.BlockSpec((planes, lanes, width), lambda i: (0, 0, i))
        out_shape = jax.ShapeDtypeStruct((planes, lanes, trials), F32)
    out = pl.pallas_call(
        functools.partial(trial_kernel, last, nfreq, frames),
        grid=(trials // width,),
        in_specs=in_specs,
        out_specs=out_spec,
        out_shape=out_shape,
        compiler_params=PARAMS,
        cost_estimate=pl.CostEstimate(
            flops=8 * planes * count * depth * lanes * trials,
            bytes_accessed=8 * count * depth * trials + 4 * planes * lanes * trials,
            transcendentals=0,
        ),
        name="dedisperse_last" if last else "dedisperse",
    )(*args)
    return out.reshape(beams, frames, trials) if last else out


def body(devices, raw, cell_feed, dm_delay):
    feeds, frames, samples = raw.shape
    nfreq = samples // 2
    chunks = math.gcd(4, nfreq // devices)
    freqs = nfreq // (devices * chunks)
    per = cell_feed.shape[0] // devices
    fast = (
        feeds == 128 and per == 64 and freqs % 16 == 0 and frames == 16 and devices % 8 == 0
    )
    table = channel_rows(samples, chunks)
    exchange = lambda v: lax.all_to_all(v, "wide", split_axis=0, concat_axis=0, tiled=True)
    hold = lax.optimization_barrier
    spectra = lambda c: channelise(rows, jnp.asarray(table[c]), devices, frames, fast)
    rows = reorder(raw, fast)
    first = spectra(0)
    rows, first = hold((rows, first))
    arrived = [exchange(first)]
    sent = [spectra(c) for c in range(1, min(2, chunks))]
    cell_feed, dm_delay, sent = hold((cell_feed, dm_delay, sent))
    matrix = sky_matrix(cell_feed, devices, fast)
    angle = (jnp.transpose(dm_delay) % frames).astype(F32) * (2.0 * math.pi / frames)
    cosine, sine = jnp.cos(angle), jnp.sin(angle)
    harmonics = []
    for c in range(1, chunks):
        arrived[-1], sent[c - 1], matrix, cosine, sine = hold(
            (arrived[-1], sent[c - 1], matrix, cosine, sine)
        )
        arrived.append(exchange(sent[c - 1]))
        if c + 1 < chunks:
            sent.append(spectra(c + 1))
        harmonics.append(beamform(arrived[c - 1], matrix, fast))
        if c + 1 < chunks:
            sent[c], harmonics[-1] = hold((sent[c], harmonics[-1]))
    total = None
    if harmonics:
        early = jnp.stack(harmonics, axis=1)
        early, arrived[-1] = hold((early, arrived[-1]))
        early = exchange(early)
    late = beamform(arrived[-1], matrix, fast)
    if harmonics:
        late, early = hold((late, early))
    late = exchange(late)[:, None]
    if harmonics:
        total = dedisperse(early, cosine, sine, 0, None, False, nfreq, frames, fast)
    return dedisperse(late, cosine, sine, chunks - 1, total, True, nfreq, frames, fast)


def solution(mesh):
    placed = (P(("grp", "wide"), None, None), P(), P())
    return jax.shard_map(
        functools.partial(body, mesh.shape["wide"]),
        mesh=mesh,
        in_specs=placed,
        out_specs=P(("grp", "wide"), None, None),
        check_vma=False,
    )
```

```python
import functools
import math

import jax
import jax.numpy as jnp
import ml_dtypes
import numpy as np
from jax import lax
from jax.experimental import pallas as pl
from jax.experimental.pallas import tpu as pltpu
from jax.sharding import PartitionSpec as P

BF16 = jnp.bfloat16
F32 = jnp.float32
PARAMS = pltpu.CompilerParams(vmem_limit_bytes=56 * 2**20)


def channel_rows(samples, chunks):
    nfreq = samples // 2
    turns = (np.arange(nfreq)[:, None] * np.arange(samples)[None, :]) % samples
    angle = turns * (2.0 * math.pi / samples)
    table = np.stack([np.cos(angle), -np.sin(angle)]) / math.sqrt(samples)
    table = table.reshape(2, chunks, nfreq // chunks, samples).transpose(1, 0, 2, 3)
    return table.reshape(chunks, -1, samples).astype(ml_dtypes.bfloat16)


def frame_factors(frames):
    angle = 2.0 * math.pi * (np.outer(np.arange(frames), np.arange(frames)) % frames) / frames
    rounded = lambda v: np.round(v, 12).astype(ml_dtypes.bfloat16).astype(np.float64)
    return rounded(np.cos(angle)), rounded(-np.sin(angle))


def sky_kernel(cosine_ref, sine_ref, row_ref, col_ref, out_ref):
    per = row_ref.shape[0]
    cells = cosine_ref.shape[0]
    here = lax.broadcasted_iota(jnp.int32, (per, cells), 1) == row_ref[...]
    pick = jnp.where(here, 1.0, 0.0).astype(BF16)
    cosine = jnp.dot(pick, cosine_ref[...], preferred_element_type=F32)
    minus = -jnp.dot(pick, sine_ref[...], preferred_element_type=F32)
    for part in range(2):
        for out in range(2):
            for q in range(4):
                turn = (col_ref[...] * q + (out - part + 4)) & 3
                turn = jnp.broadcast_to(turn, cosine.shape)
                value = jnp.where((turn & 1) == 1, minus, cosine)
                value = jnp.where(turn >= 2, -value, value).astype(BF16)
                at = (out * 4 + q) * cells
                out_ref[part * per : (part + 1) * per, at : at + cells] = value


def sky_matrix(cell_feed, devices, fast):
    total = cell_feed.shape[0]
    cells = total // 4
    per = total // devices
    places = lax.broadcasted_iota(jnp.int32, (total, total), 1)
    feeds = lax.broadcasted_iota(jnp.int32, (total, total), 0)
    cell = jnp.sum(jnp.where(cell_feed[None, :] == feeds, places, 0), axis=1, keepdims=True)
    row = cell % cells
    col = cell // cells
    if fast:
        turns = np.outer(np.arange(cells), np.arange(cells)) % cells
        angle = turns * (2.0 * math.pi / cells)
        tables = [
            jnp.asarray((wave(angle) / math.sqrt(cells)).astype(ml_dtypes.bfloat16))
            for wave in (np.cos, np.sin)
        ]
        return pl.pallas_call(
            sky_kernel,
            grid=(devices,),
            in_specs=[
                pl.BlockSpec((cells, cells), lambda i: (0, 0)),
                pl.BlockSpec((cells, cells), lambda i: (0, 0)),
                pl.BlockSpec((per, 1), lambda i: (i, 0)),
                pl.BlockSpec((per, 1), lambda i: (i, 0)),
            ],
            out_specs=pl.BlockSpec((2 * per, 2 * total), lambda i: (i, 0)),
            out_shape=jax.ShapeDtypeStruct((2 * total, 2 * total), BF16),
            compiler_params=PARAMS,
            name="sky",
        )(*tables, row, col)
    row = row.reshape(devices, 1, per, 1, 1)
    col = col.reshape(devices, 1, per, 1, 1)
    shape = (devices, 2, per, 2, total)
    beam = lax.broadcasted_iota(jnp.int32, (1, 1, 1, 1, total), 4)
    part_in = lax.broadcasted_iota(jnp.int32, (1, 2, 1, 1, 1), 1)
    part_out = lax.broadcasted_iota(jnp.int32, (1, 1, 1, 2, 1), 3)
    quarter = cells // 4
    turns = (beam % cells) * row + quarter * ((beam // cells) * col + part_out - part_in + 4)
    angle = (turns % cells).astype(F32) * (2.0 * math.pi / cells)
    table = (jnp.cos(angle) * (1.0 / math.sqrt(cells))).astype(BF16)
    return jnp.broadcast_to(table, shape).reshape(2 * total, 2 * total)


def split_halves(a, b):
    half = a.shape[-1] // 2
    low = lax.broadcasted_iota(jnp.int32, a.shape, a.ndim - 1) < half
    return (
        jnp.where(low, a, pltpu.roll(b, half, a.ndim - 1)),
        jnp.where(low, pltpu.roll(a, half, a.ndim - 1), b),
    )


def reorder_kernel(perm_ref, raw_ref, out_ref):
    block, frames, samples = raw_ref.shape
    size = perm_ref.shape[0]
    rows = raw_ref[...].reshape(block * frames, samples)
    parts = [
        jnp.dot(perm_ref[...], rows[at : at + size], preferred_element_type=F32)
        for at in range(0, block * frames, size)
    ]
    parts = [v.reshape(2 * frames, size // (2 * frames), samples) for v in parts]
    moved = jnp.concatenate(parts, axis=1).astype(BF16)
    out_ref[...] = moved.reshape(out_ref.shape)


def reorder(raw, fast):
    feeds, frames, samples = raw.shape
    ants = feeds // 2
    if not fast:
        out = raw.reshape(ants, 2, frames, samples).transpose(2, 1, 0, 3)
        return out.reshape(feeds * frames, samples)
    block = 16
    size = block * frames
    target = np.arange(size).reshape(block // 2, 2, frames).transpose(2, 1, 0).reshape(-1)
    perm = np.zeros((size, size), ml_dtypes.bfloat16)
    perm[np.arange(size), target] = 1
    width = samples // 2
    out = pl.pallas_call(
        reorder_kernel,
        grid=(ants // block, 2),
        in_specs=[
            pl.BlockSpec((size, size), lambda i, j: (0, 0)),
            pl.BlockSpec((2 * block, frames, width), lambda i, j: (i, 0, j)),
        ],
        out_specs=pl.BlockSpec((frames, 2, block, width), lambda i, j: (0, 0, i, j)),
        out_shape=jax.ShapeDtypeStruct((frames, 2, ants, samples), BF16),
        compiler_params=PARAMS,
        name="reorder",
    )(jnp.asarray(perm), raw)
    return out.reshape(feeds * frames, samples)


def channel_kernel(table_ref, rows_ref, out_ref):
    devices, _, frames, freqs, lanes = out_ref.shape
    half = table_ref.shape[0] // 2
    whole = lax.dot_general(
        table_ref[...], rows_ref[...], (((1,), (1,)), ((), ())), preferred_element_type=F32
    )
    for r in range(frames):
        spec = whole[:, r * lanes : (r + 1) * lanes]
        pair = split_halves(spec[:half], spec[half:])
        for p in range(2):
            out_ref[:, p, r] = pair[p].astype(BF16).reshape(devices, freqs, lanes)


def channelise(rows, table, devices, frames, fast):
    total, samples = rows.shape
    ants = total // (2 * frames)
    freqs = table.shape[0] // (2 * devices)
    if not fast:
        spec = lax.dot_general(
            table, rows, (((1,), (1,)), ((), ())), preferred_element_type=F32
        ).astype(BF16)
        spec = spec.reshape(2, devices, freqs, frames, 2, ants).transpose(1, 4, 3, 2, 0, 5)
        return spec.reshape(devices, 2, frames, freqs, 2 * ants)
    block = 4
    return pl.pallas_call(
        channel_kernel,
        grid=(frames // block,),
        in_specs=[
            pl.BlockSpec(table.shape, lambda i: (0, 0)),
            pl.BlockSpec((block * 2 * ants, samples), lambda i: (i, 0)),
        ],
        out_specs=pl.BlockSpec(
            (devices, 2, block, freqs, 2 * ants), lambda i: (0, 0, i, 0, 0)
        ),
        out_shape=jax.ShapeDtypeStruct((devices, 2, frames, freqs, 2 * ants), BF16),
        compiler_params=PARAMS,
        name="channelise",
    )(table, rows)


def harmonics_of(power, frames):
    mean = functools.reduce(lambda x, y: x + y, power) * (1.0 / frames)
    rows = [(v - mean).astype(BF16).astype(F32) for v in power]
    cosine, sine = frame_factors(frames)

    def total(weights):
        terms = [float(w) * v for w, v in zip(weights, rows) if w != 0]
        return functools.reduce(lambda x, y: x + y, terms)

    planes = [(total(cosine[0]), total(cosine[frames // 2]))]
    for h in range(1, frames // 2):
        planes.append((total(cosine[h]), total(sine[h])))
    return planes


def beam_kernel(spec_ref, real_ref, imag_ref, out_ref, left):
    devices, _, frames, freqs, lanes = spec_ref.shape
    rows = 2 * frames * freqs

    @pl.when(pl.program_id(0) == 0)
    def _():
        for w in range(devices):
            left[:, w * lanes : (w + 1) * lanes] = spec_ref[w].reshape(rows, lanes)

    real = jnp.dot(left[...], real_ref[...], preferred_element_type=F32)
    imag = jnp.dot(left[...], imag_ref[...], preferred_element_type=F32)
    square = (real * real + imag * imag).reshape(2, frames, freqs, -1)
    power = (square[0] + square[1]) * 0.125
    planes = harmonics_of([power[r] for r in range(frames)], frames)
    for h, (a, b) in enumerate(planes):
        for g in range(out_ref.shape[0] // 2):
            cut = slice(g * lanes, (g + 1) * lanes)
            first, second = split_halves(a[:, cut], b[:, cut])
            out_ref[2 * g, h] = first.astype(BF16)
            out_ref[2 * g + 1, h] = second.astype(BF16)


def beamform(spec, matrix, fast):
    devices, _, frames, freqs, lanes = spec.shape
    total = matrix.shape[1] // 2
    per = total // devices
    planes = frames // 2
    if not fast:
        beams = jnp.einsum(
            "wprfx,wxub->prfub",
            spec,
            matrix.reshape(devices, lanes, 2, total),
            preferred_element_type=F32,
        )
        power = 0.125 * jnp.sum(beams * beams, axis=(0, 3))
        found = harmonics_of([power[r] for r in range(frames)], frames)
        out = jnp.stack([jnp.stack(pair) for pair in found]).astype(BF16)
        out = out.reshape(planes, 2, freqs, devices, per).transpose(3, 0, 2, 1, 4)
        return out.reshape(devices, planes, freqs, 2 * per)
    steps = 4
    width = total // steps
    return pl.pallas_call(
        beam_kernel,
        grid=(steps,),
        in_specs=[
            pl.BlockSpec(spec.shape, lambda i: (0, 0, 0, 0, 0)),
            pl.BlockSpec((matrix.shape[0], width), lambda i: (0, i)),
            pl.BlockSpec((matrix.shape[0], width), lambda i: (0, i + steps)),
        ],
        out_specs=pl.BlockSpec(
            (devices // steps, planes, freqs, 2 * per), lambda i: (i, 0, 0, 0)
        ),
        out_shape=jax.ShapeDtypeStruct((devices, planes, freqs, 2 * per), BF16),
        scratch_shapes=[pltpu.VMEM((2 * frames * freqs, devices * lanes), BF16)],
        compiler_params=PARAMS,
        name="beamform",
    )(spec, matrix, matrix)


def plane_factors(cosine, sine, planes):
    now = (cosine, sine)
    found = []
    for _ in range(1, planes):
        found.append((now[0].astype(BF16), now[1].astype(BF16)))
        c, s = now
        now = (c * cosine - s * sine, s * cosine + c * sine)
    return [(jnp.ones(cosine.shape, BF16), now[0].astype(BF16))] + found


def factor_kernel(cos_ref, sin_ref, out_ref):
    for h, pair in enumerate(plane_factors(cos_ref[...], sin_ref[...], out_ref.shape[0])):
        out_ref[h, 0] = pair[0]
        out_ref[h, 1] = pair[1]


def trial_factors(cosine, sine, planes, fast):
    if not fast:
        return jnp.stack([jnp.stack(pair) for pair in plane_factors(cosine, sine, planes)])
    nfreq, trials = cosine.shape
    depth = math.gcd(nfreq, 64)
    return pl.pallas_call(
        factor_kernel,
        grid=(nfreq // depth,),
        in_specs=[pl.BlockSpec((depth, trials), lambda i: (i, 0))] * 2,
        out_specs=pl.BlockSpec((planes, 2, depth, trials), lambda i: (0, 0, i, 0)),
        out_shape=jax.ShapeDtypeStruct((planes, 2, nfreq, trials), BF16),
        compiler_params=PARAMS,
        name="factors",
    )(cosine, sine)


def trial_planes(block, factors, before):
    devices, planes, freqs, lanes = block.shape
    half = lanes // 2
    low = lax.broadcasted_iota(jnp.int32, (devices * freqs, lanes), 1) < half
    result = []
    for h in range(planes):
        left = block[:, h].reshape(devices * freqs, lanes).astype(F32)
        if h:
            other = jnp.concatenate([-left[:, half:], left[:, :half]], axis=1)
        else:
            other = jnp.where(low, 0.0, left)
            left = jnp.where(low, left, 0.0)
        sums = lax.dot_general(
            jnp.concatenate([left, other], axis=0).astype(BF16),
            jnp.concatenate([factors[h, 0], factors[h, 1]], axis=0),
            (((0,), (0,)), ((), ())),
            preferred_element_type=F32,
        )
        result.append(sums if before is None else sums + before[h])
    return result


def synthesis(planes, frames, nfreq):
    half = planes[0].shape[0] // 2
    scale = 1.0 / (frames * math.sqrt(nfreq))
    middle = frames // 2
    real = {0: planes[0][:half] * scale, middle: planes[0][half:] * scale}
    imag = {}
    for h in range(1, middle):
        real[h] = planes[h][:half] * (2.0 * scale)
        imag[h] = planes[h][half:] * (2.0 * scale)
    add = lambda terms: functools.reduce(lambda x, y: x + y, terms)

    def weighted(values, t, parity, wave):
        found = []
        for h, v in values.items():
            factor = round(wave(2.0 * math.pi * ((h * t) % frames) / frames), 15)
            if h % 2 == parity and factor != 0:
                found.append(v if factor == 1 else -v if factor == -1 else v * factor)
        return add(found) if found else jnp.zeros_like(real[0])

    out = [None] * frames
    for t in range(middle // 2 + 1):
        even, odd = (weighted(real, t, p, math.cos) for p in range(2))
        even_s, odd_s = (weighted(imag, t, p, math.sin) for p in range(2))
        for at, a, b in ((t, even + odd, even_s + odd_s), (middle - t, even - odd, odd_s - even_s)):
            out[at] = a - b
            out[(frames - at) % frames] = a + b if at % middle else a - b
    return out


def trial_kernel(last, nfreq, frames, *refs):
    block_ref, factor_ref, *rest = refs
    found = rest[0] if len(rest) == 2 else None
    out_ref = rest[-1]
    devices, count, _, freqs, _ = block_ref.shape
    depth = devices * freqs
    for c in range(count):
        cut = slice(c * depth, (c + 1) * depth)
        found = trial_planes(block_ref[:, c], factor_ref.at[:, :, cut], found)
    if not last:
        for h, plane in enumerate(found):
            out_ref[h] = plane
        return
    beams = out_ref.shape[0] // frames
    for t, series in enumerate(synthesis(found, frames, nfreq)):
        out_ref[pl.ds(t, beams, stride=frames), :] = series


def dedisperse(block, factors, first, before, last, nfreq, frames, fast):
    devices, count, planes, freqs, lanes = block.shape
    depth = devices * freqs
    trials = factors.shape[3]
    beams = lanes // 2
    if not fast:
        found = before
        for c in range(count):
            cut = slice((first + c) * depth, (first + c + 1) * depth)
            found = trial_planes(block[:, c], factors[:, :, cut], found)
        if not last:
            return jnp.stack(found)
        return jnp.stack(synthesis(found, frames, nfreq), axis=1)
    width = min(128 if last else 256, trials)
    at = first // count
    in_specs = [
        pl.BlockSpec(block.shape, lambda i: (0, 0, 0, 0, 0)),
        pl.BlockSpec((planes, 2, count * depth, width), lambda i: (0, 0, at, i)),
    ]
    args = [block, factors]
    if before is not None:
        in_specs.append(pl.BlockSpec((planes, lanes, width), lambda i: (0, 0, i)))
        args.append(before)
    if last:
        out_spec = pl.BlockSpec((beams * frames, width), lambda i: (0, i))
        out_shape = jax.ShapeDtypeStruct((beams * frames, trials), F32)
    else:
        out_spec = pl.BlockSpec((planes, lanes, width), lambda i: (0, 0, i))
        out_shape = jax.ShapeDtypeStruct((planes, lanes, trials), F32)
    out = pl.pallas_call(
        functools.partial(trial_kernel, last, nfreq, frames),
        grid=(trials // width,),
        in_specs=in_specs,
        out_specs=out_spec,
        out_shape=out_shape,
        compiler_params=PARAMS,
        cost_estimate=pl.CostEstimate(
            flops=8 * planes * count * depth * lanes * trials,
            bytes_accessed=4 * planes * count * depth * trials + 4 * planes * lanes * trials,
            transcendentals=0,
        ),
        name="dedisperse_last" if last else "dedisperse",
    )(*args)
    return out.reshape(beams, frames, trials) if last else out


def body(devices, raw, cell_feed, dm_delay):
    feeds, frames, samples = raw.shape
    nfreq = samples // 2
    chunks = math.gcd(4, nfreq // devices)
    freqs = nfreq // (devices * chunks)
    per = cell_feed.shape[0] // devices
    fast = (
        feeds == 128 and per == 64 and freqs % 16 == 0 and frames == 16 and devices % 8 == 0
    )
    table = channel_rows(samples, chunks)
    exchange = lambda v: lax.all_to_all(v, "wide", split_axis=0, concat_axis=0, tiled=True)
    hold = lax.optimization_barrier
    spectra = lambda c: channelise(rows, jnp.asarray(table[c]), devices, frames, fast)
    rows = reorder(raw, fast)
    first = spectra(0)
    rows, first = hold((rows, first))
    arrived = [exchange(first)]
    sent = [spectra(c) for c in range(1, min(2, chunks))]
    cell_feed, dm_delay, sent = hold((cell_feed, dm_delay, sent))
    matrix = sky_matrix(cell_feed, devices, fast)
    angle = (jnp.transpose(dm_delay) % frames).astype(F32) * (2.0 * math.pi / frames)
    cosine, sine = jnp.cos(angle), jnp.sin(angle)
    harmonics = []
    factors = trial_factors(cosine, sine, frames // 2, fast) if chunks == 1 else None
    for c in range(1, chunks):
        arrived[-1], sent[c - 1], matrix, cosine, sine = hold(
            (arrived[-1], sent[c - 1], matrix, cosine, sine)
        )
        arrived.append(exchange(sent[c - 1]))
        if c + 1 < chunks:
            sent.append(spectra(c + 1))
        harmonics.append(beamform(arrived[c - 1], matrix, fast))
        if c == 1:
            factors = trial_factors(cosine, sine, frames // 2, fast)
            harmonics[-1], factors = hold((harmonics[-1], factors))
        if c + 1 < chunks:
            sent[c], harmonics[-1] = hold((sent[c], harmonics[-1]))
    total = None
    if harmonics:
        early = jnp.stack(harmonics, axis=1)
        early, arrived[-1] = hold((early, arrived[-1]))
        early = exchange(early)
    late = beamform(arrived[-1], matrix, fast)
    if harmonics:
        late, early = hold((late, early))
    late = exchange(late)[:, None]
    if harmonics:
        total = dedisperse(early, factors, 0, None, False, nfreq, frames, fast)
    return dedisperse(late, factors, chunks - 1, total, True, nfreq, frames, fast)


def solution(mesh):
    placed = (P(("grp", "wide"), None, None), P(), P())
    return jax.shard_map(
        functools.partial(body, mesh.shape["wide"]),
        mesh=mesh,
        in_specs=placed,
        out_specs=P(("grp", "wide"), None, None),
        check_vma=False,
    )
```

```python
import functools
import math

import jax
import jax.numpy as jnp
import ml_dtypes
import numpy as np
from jax import lax
from jax.experimental import pallas as pl
from jax.experimental.pallas import tpu as pltpu
from jax.sharding import PartitionSpec as P

BF16 = jnp.bfloat16
F32 = jnp.float32
PARAMS = pltpu.CompilerParams(vmem_limit_bytes=56 * 2**20)


def channel_rows(samples, sizes):
    nfreq = samples // 2
    turns = (np.arange(nfreq)[:, None] * np.arange(samples)[None, :]) % samples
    angle = turns * (2.0 * math.pi / samples)
    table = np.stack([np.cos(angle), -np.sin(angle)]) / math.sqrt(samples)
    table = table.astype(ml_dtypes.bfloat16)
    parts = np.split(table, np.cumsum(sizes)[:-1], axis=1)
    return [part.reshape(-1, samples) for part in parts]


def frame_factors(frames):
    angle = 2.0 * math.pi * (np.outer(np.arange(frames), np.arange(frames)) % frames) / frames
    rounded = lambda v: np.round(v, 12).astype(ml_dtypes.bfloat16).astype(np.float64)
    return rounded(np.cos(angle)), rounded(-np.sin(angle))


def sky_kernel(cosine_ref, sine_ref, row_ref, col_ref, out_ref):
    per = row_ref.shape[0]
    cells = cosine_ref.shape[0]
    here = lax.broadcasted_iota(jnp.int32, (per, cells), 1) == row_ref[...]
    pick = jnp.where(here, 1.0, 0.0).astype(BF16)
    cosine = jnp.dot(pick, cosine_ref[...], preferred_element_type=F32)
    minus = -jnp.dot(pick, sine_ref[...], preferred_element_type=F32)
    for part in range(2):
        for out in range(2):
            for q in range(4):
                turn = (col_ref[...] * q + (out - part + 4)) & 3
                turn = jnp.broadcast_to(turn, cosine.shape)
                value = jnp.where((turn & 1) == 1, minus, cosine)
                value = jnp.where(turn >= 2, -value, value).astype(BF16)
                at = (out * 4 + q) * cells
                out_ref[part * per : (part + 1) * per, at : at + cells] = value


def sky_matrix(cell_feed, devices, fast):
    total = cell_feed.shape[0]
    cells = total // 4
    per = total // devices
    places = lax.broadcasted_iota(jnp.int32, (total, total), 1)
    feeds = lax.broadcasted_iota(jnp.int32, (total, total), 0)
    cell = jnp.sum(jnp.where(cell_feed[None, :] == feeds, places, 0), axis=1, keepdims=True)
    row = cell % cells
    col = cell // cells
    if fast:
        turns = np.outer(np.arange(cells), np.arange(cells)) % cells
        angle = turns * (2.0 * math.pi / cells)
        tables = [
            jnp.asarray((wave(angle) / math.sqrt(cells)).astype(ml_dtypes.bfloat16))
            for wave in (np.cos, np.sin)
        ]
        return pl.pallas_call(
            sky_kernel,
            grid=(devices,),
            in_specs=[
                pl.BlockSpec((cells, cells), lambda i: (0, 0)),
                pl.BlockSpec((cells, cells), lambda i: (0, 0)),
                pl.BlockSpec((per, 1), lambda i: (i, 0)),
                pl.BlockSpec((per, 1), lambda i: (i, 0)),
            ],
            out_specs=pl.BlockSpec((2 * per, 2 * total), lambda i: (i, 0)),
            out_shape=jax.ShapeDtypeStruct((2 * total, 2 * total), BF16),
            compiler_params=PARAMS,
            name="sky",
        )(*tables, row, col)
    row = row.reshape(devices, 1, per, 1, 1)
    col = col.reshape(devices, 1, per, 1, 1)
    shape = (devices, 2, per, 2, total)
    beam = lax.broadcasted_iota(jnp.int32, (1, 1, 1, 1, total), 4)
    part_in = lax.broadcasted_iota(jnp.int32, (1, 2, 1, 1, 1), 1)
    part_out = lax.broadcasted_iota(jnp.int32, (1, 1, 1, 2, 1), 3)
    quarter = cells // 4
    turns = (beam % cells) * row + quarter * ((beam // cells) * col + part_out - part_in + 4)
    angle = (turns % cells).astype(F32) * (2.0 * math.pi / cells)
    table = (jnp.cos(angle) * (1.0 / math.sqrt(cells))).astype(BF16)
    return jnp.broadcast_to(table, shape).reshape(2 * total, 2 * total)


def split_halves(a, b):
    half = a.shape[-1] // 2
    low = lax.broadcasted_iota(jnp.int32, a.shape, a.ndim - 1) < half
    return (
        jnp.where(low, a, pltpu.roll(b, half, a.ndim - 1)),
        jnp.where(low, pltpu.roll(a, half, a.ndim - 1), b),
    )


def reorder_kernel(perm_ref, raw_ref, out_ref):
    block, frames, samples = raw_ref.shape
    size = perm_ref.shape[0]
    rows = raw_ref[...].reshape(block * frames, samples)
    parts = [
        jnp.dot(perm_ref[...], rows[at : at + size], preferred_element_type=F32)
        for at in range(0, block * frames, size)
    ]
    parts = [v.reshape(2 * frames, size // (2 * frames), samples) for v in parts]
    moved = jnp.concatenate(parts, axis=1).astype(BF16)
    out_ref[...] = moved.reshape(out_ref.shape)


def reorder(raw, fast):
    feeds, frames, samples = raw.shape
    ants = feeds // 2
    if not fast:
        out = raw.reshape(ants, 2, frames, samples).transpose(2, 1, 0, 3)
        return out.reshape(feeds * frames, samples)
    block = 16
    size = block * frames
    target = np.arange(size).reshape(block // 2, 2, frames).transpose(2, 1, 0).reshape(-1)
    perm = np.zeros((size, size), ml_dtypes.bfloat16)
    perm[np.arange(size), target] = 1
    width = samples // 2
    out = pl.pallas_call(
        reorder_kernel,
        grid=(ants // block, 2),
        in_specs=[
            pl.BlockSpec((size, size), lambda i, j: (0, 0)),
            pl.BlockSpec((2 * block, frames, width), lambda i, j: (i, 0, j)),
        ],
        out_specs=pl.BlockSpec((frames, 2, block, width), lambda i, j: (0, 0, i, j)),
        out_shape=jax.ShapeDtypeStruct((frames, 2, ants, samples), BF16),
        compiler_params=PARAMS,
        name="reorder",
    )(jnp.asarray(perm), raw)
    return out.reshape(feeds * frames, samples)


def channel_kernel(table_ref, rows_ref, out_ref):
    devices, _, frames, freqs, lanes = out_ref.shape
    half = table_ref.shape[0] // 2
    whole = lax.dot_general(
        table_ref[...], rows_ref[...], (((1,), (1,)), ((), ())), preferred_element_type=F32
    )
    for r in range(frames):
        spec = whole[:, r * lanes : (r + 1) * lanes]
        pair = split_halves(spec[:half], spec[half:])
        for p in range(2):
            out_ref[:, p, r] = pair[p].astype(BF16).reshape(devices, freqs, lanes)


def channelise(rows, table, devices, frames, fast):
    total, samples = rows.shape
    ants = total // (2 * frames)
    freqs = table.shape[0] // (2 * devices)
    if not fast:
        spec = lax.dot_general(
            table, rows, (((1,), (1,)), ((), ())), preferred_element_type=F32
        ).astype(BF16)
        spec = spec.reshape(2, devices, freqs, frames, 2, ants).transpose(1, 4, 3, 2, 0, 5)
        return spec.reshape(devices, 2, frames, freqs, 2 * ants)
    block = 4
    return pl.pallas_call(
        channel_kernel,
        grid=(frames // block,),
        in_specs=[
            pl.BlockSpec(table.shape, lambda i: (0, 0)),
            pl.BlockSpec((block * 2 * ants, samples), lambda i: (i, 0)),
        ],
        out_specs=pl.BlockSpec(
            (devices, 2, block, freqs, 2 * ants), lambda i: (0, 0, i, 0, 0)
        ),
        out_shape=jax.ShapeDtypeStruct((devices, 2, frames, freqs, 2 * ants), BF16),
        compiler_params=PARAMS,
        name="channelise",
    )(table, rows)


def harmonics_of(power, frames):
    mean = functools.reduce(lambda x, y: x + y, power) * (1.0 / frames)
    rows = [(v - mean).astype(BF16).astype(F32) for v in power]
    cosine, sine = frame_factors(frames)

    def total(weights):
        terms = [float(w) * v for w, v in zip(weights, rows) if w != 0]
        return functools.reduce(lambda x, y: x + y, terms)

    planes = [(total(cosine[0]), total(cosine[frames // 2]))]
    for h in range(1, frames // 2):
        planes.append((total(cosine[h]), total(sine[h])))
    return planes


def beam_kernel(spec_ref, real_ref, imag_ref, out_ref, left):
    devices, _, frames, freqs, lanes = spec_ref.shape
    rows = 2 * frames * freqs

    @pl.when(pl.program_id(0) == 0)
    def _():
        for w in range(devices):
            left[:, w * lanes : (w + 1) * lanes] = spec_ref[w].reshape(rows, lanes)

    real = jnp.dot(left[...], real_ref[...], preferred_element_type=F32)
    imag = jnp.dot(left[...], imag_ref[...], preferred_element_type=F32)
    square = (real * real + imag * imag).reshape(2, frames, freqs, -1)
    power = (square[0] + square[1]) * 0.125
    planes = harmonics_of([power[r] for r in range(frames)], frames)
    for h, (a, b) in enumerate(planes):
        for g in range(out_ref.shape[0] // 2):
            cut = slice(g * lanes, (g + 1) * lanes)
            first, second = split_halves(a[:, cut], b[:, cut])
            out_ref[2 * g, h] = first.astype(BF16)
            out_ref[2 * g + 1, h] = second.astype(BF16)


def beamform(spec, matrix, fast):
    devices, _, frames, freqs, lanes = spec.shape
    total = matrix.shape[1] // 2
    per = total // devices
    planes = frames // 2
    if not fast:
        beams = jnp.einsum(
            "wprfx,wxub->prfub",
            spec,
            matrix.reshape(devices, lanes, 2, total),
            preferred_element_type=F32,
        )
        power = 0.125 * jnp.sum(beams * beams, axis=(0, 3))
        found = harmonics_of([power[r] for r in range(frames)], frames)
        out = jnp.stack([jnp.stack(pair) for pair in found]).astype(BF16)
        out = out.reshape(planes, 2, freqs, devices, per).transpose(3, 0, 2, 1, 4)
        return out.reshape(devices, planes, freqs, 2 * per)
    steps = 4
    width = total // steps
    return pl.pallas_call(
        beam_kernel,
        grid=(steps,),
        in_specs=[
            pl.BlockSpec(spec.shape, lambda i: (0, 0, 0, 0, 0)),
            pl.BlockSpec((matrix.shape[0], width), lambda i: (0, i)),
            pl.BlockSpec((matrix.shape[0], width), lambda i: (0, i + steps)),
        ],
        out_specs=pl.BlockSpec(
            (devices // steps, planes, freqs, 2 * per), lambda i: (i, 0, 0, 0)
        ),
        out_shape=jax.ShapeDtypeStruct((devices, planes, freqs, 2 * per), BF16),
        scratch_shapes=[pltpu.VMEM((2 * frames * freqs, devices * lanes), BF16)],
        compiler_params=PARAMS,
        name="beamform",
    )(spec, matrix, matrix)


def plane_factors(cosine, sine, planes):
    now = (cosine, sine)
    found = []
    for _ in range(1, planes):
        found.append((now[0].astype(BF16), now[1].astype(BF16)))
        c, s = now
        now = (c * cosine - s * sine, s * cosine + c * sine)
    return [(jnp.ones(cosine.shape, BF16), now[0].astype(BF16))] + found


def factor_kernel(cos_ref, sin_ref, out_ref):
    for h, pair in enumerate(plane_factors(cos_ref[...], sin_ref[...], out_ref.shape[0])):
        out_ref[h, 0] = pair[0]
        out_ref[h, 1] = pair[1]


def trial_factors(cosine, sine, planes, fast):
    if not fast:
        return jnp.stack([jnp.stack(pair) for pair in plane_factors(cosine, sine, planes)])
    nfreq, trials = cosine.shape
    depth = math.gcd(nfreq, 64)
    return pl.pallas_call(
        factor_kernel,
        grid=(nfreq // depth,),
        in_specs=[pl.BlockSpec((depth, trials), lambda i: (i, 0))] * 2,
        out_specs=pl.BlockSpec((planes, 2, depth, trials), lambda i: (0, 0, i, 0)),
        out_shape=jax.ShapeDtypeStruct((planes, 2, nfreq, trials), BF16),
        compiler_params=PARAMS,
        name="factors",
    )(cosine, sine)


def trial_planes(block, factors, before):
    devices, planes, freqs, lanes = block.shape
    half = lanes // 2
    low = lax.broadcasted_iota(jnp.int32, (devices * freqs, lanes), 1) < half
    result = []
    for h in range(planes):
        left = block[:, h].reshape(devices * freqs, lanes).astype(F32)
        if h:
            other = jnp.concatenate([-left[:, half:], left[:, :half]], axis=1)
        else:
            other = jnp.where(low, 0.0, left)
            left = jnp.where(low, left, 0.0)
        sums = lax.dot_general(
            jnp.concatenate([left, other], axis=0).astype(BF16),
            jnp.concatenate([factors[h, 0], factors[h, 1]], axis=0),
            (((0,), (0,)), ((), ())),
            preferred_element_type=F32,
        )
        result.append(sums if before is None else sums + before[h])
    return result


def synthesis(planes, frames, nfreq):
    half = planes[0].shape[0] // 2
    scale = 1.0 / (frames * math.sqrt(nfreq))
    middle = frames // 2
    real = {0: planes[0][:half] * scale, middle: planes[0][half:] * scale}
    imag = {}
    for h in range(1, middle):
        real[h] = planes[h][:half] * (2.0 * scale)
        imag[h] = planes[h][half:] * (2.0 * scale)
    add = lambda terms: functools.reduce(lambda x, y: x + y, terms)

    def weighted(values, t, parity, wave):
        found = []
        for h, v in values.items():
            factor = round(wave(2.0 * math.pi * ((h * t) % frames) / frames), 15)
            if h % 2 == parity and factor != 0:
                found.append(v if factor == 1 else -v if factor == -1 else v * factor)
        return add(found) if found else jnp.zeros_like(real[0])

    out = [None] * frames
    for t in range(middle // 2 + 1):
        even, odd = (weighted(real, t, p, math.cos) for p in range(2))
        even_s, odd_s = (weighted(imag, t, p, math.sin) for p in range(2))
        for at, a, b in ((t, even + odd, even_s + odd_s), (middle - t, even - odd, odd_s - even_s)):
            out[at] = a - b
            out[(frames - at) % frames] = a + b if at % middle else a - b
    return out


def trial_kernel(last, nfreq, frames, sizes, *refs):
    block_ref, factor_ref, *rest = refs
    found = rest[0] if len(rest) == 2 else None
    out_ref = rest[-1]
    devices = block_ref.shape[0]
    at = 0
    for size in sizes:
        part = block_ref[:, :, at : at + size]
        cut = slice(at * devices, (at + size) * devices)
        found = trial_planes(part, factor_ref.at[:, :, cut], found)
        at += size
    if not last:
        for h, plane in enumerate(found):
            out_ref[h] = plane
        return
    beams = out_ref.shape[0] // frames
    for t, series in enumerate(synthesis(found, frames, nfreq)):
        out_ref[pl.ds(t, beams, stride=frames), :] = series


def dedisperse(block, sizes, factors, first, before, last, nfreq, frames, fast):
    devices, planes, freqs, lanes = block.shape
    depth = devices * freqs
    trials = factors.shape[3]
    beams = lanes // 2
    if not fast:
        found = before
        at = 0
        for size in sizes:
            cut = slice(first + at * devices, first + (at + size) * devices)
            found = trial_planes(block[:, :, at : at + size], factors[:, :, cut], found)
            at += size
        if not last:
            return jnp.stack(found)
        return jnp.stack(synthesis(found, frames, nfreq), axis=1)
    width = min(128 if last else 256, trials)
    at = first // depth
    in_specs = [
        pl.BlockSpec(block.shape, lambda i: (0, 0, 0, 0)),
        pl.BlockSpec((planes, 2, depth, width), lambda i: (0, 0, at, i)),
    ]
    args = [block, factors]
    if before is not None:
        in_specs.append(pl.BlockSpec((planes, lanes, width), lambda i: (0, 0, i)))
        args.append(before)
    if last:
        out_spec = pl.BlockSpec((beams * frames, width), lambda i: (0, i))
        out_shape = jax.ShapeDtypeStruct((beams * frames, trials), F32)
    else:
        out_spec = pl.BlockSpec((planes, lanes, width), lambda i: (0, 0, i))
        out_shape = jax.ShapeDtypeStruct((planes, lanes, trials), F32)
    out = pl.pallas_call(
        functools.partial(trial_kernel, last, nfreq, frames, sizes),
        grid=(trials // width,),
        in_specs=in_specs,
        out_specs=out_spec,
        out_shape=out_shape,
        compiler_params=PARAMS,
        cost_estimate=pl.CostEstimate(
            flops=8 * planes * depth * lanes * trials,
            bytes_accessed=4 * planes * depth * trials + 4 * planes * lanes * trials,
            transcendentals=0,
        ),
        name="dedisperse_last" if last else "dedisperse",
    )(*args)
    return out.reshape(beams, frames, trials) if last else out


def body(devices, raw, cell_feed, dm_delay):
    feeds, frames, samples = raw.shape
    nfreq = samples // 2
    freqs = nfreq // (devices * math.gcd(4, nfreq // devices))
    sizes = [freqs] * math.gcd(4, nfreq // devices)
    if len(sizes) == 4:
        sizes = [freqs, 2 * freqs, freqs]
    chunks = len(sizes)
    per = cell_feed.shape[0] // devices
    fast = (
        feeds == 128 and per == 64 and freqs % 16 == 0 and frames == 16 and devices % 8 == 0
    )
    table = channel_rows(samples, [devices * size for size in sizes])
    exchange = lambda v: lax.all_to_all(v, "wide", split_axis=0, concat_axis=0, tiled=True)
    hold = lax.optimization_barrier
    spectra = lambda c: channelise(rows, jnp.asarray(table[c]), devices, frames, fast)
    rows = reorder(raw, fast)
    first = spectra(0)
    rows, first = hold((rows, first))
    arrived = [exchange(first)]
    sent = [spectra(c) for c in range(1, min(2, chunks))]
    cell_feed, dm_delay, sent = hold((cell_feed, dm_delay, sent))
    matrix = sky_matrix(cell_feed, devices, fast)
    angle = (jnp.transpose(dm_delay) % frames).astype(F32) * (2.0 * math.pi / frames)
    cosine, sine = jnp.cos(angle), jnp.sin(angle)
    harmonics = []
    factors = trial_factors(cosine, sine, frames // 2, fast) if chunks == 1 else None
    for c in range(1, chunks):
        arrived[-1], sent[c - 1], matrix, cosine, sine = hold(
            (arrived[-1], sent[c - 1], matrix, cosine, sine)
        )
        arrived.append(exchange(sent[c - 1]))
        if c + 1 < chunks:
            sent.append(spectra(c + 1))
        harmonics.append(beamform(arrived[c - 1], matrix, fast))
        if c == 1:
            factors = trial_factors(cosine, sine, frames // 2, fast)
            harmonics[-1], factors = hold((harmonics[-1], factors))
        if c + 1 < chunks:
            sent[c], harmonics[-1] = hold((sent[c], harmonics[-1]))
    total = None
    if harmonics:
        early = jnp.concatenate(harmonics, axis=2)
        early, arrived[-1] = hold((early, arrived[-1]))
        early = exchange(early)
    late = beamform(arrived[-1], matrix, fast)
    if harmonics:
        late, early = hold((late, early))
    late = exchange(late)
    if harmonics:
        total = dedisperse(early, sizes[:-1], factors, 0, None, False, nfreq, frames, fast)
    start = nfreq - devices * sizes[-1]
    return dedisperse(late, sizes[-1:], factors, start, total, True, nfreq, frames, fast)


def solution(mesh):
    placed = (P(("grp", "wide"), None, None), P(), P())
    return jax.shard_map(
        functools.partial(body, mesh.shape["wide"]),
        mesh=mesh,
        in_specs=placed,
        out_specs=P(("grp", "wide"), None, None),
        check_vma=False,
    )
```
